32 devices in a mesh: dom: 2 (over y), slab: 16 (over z, x, core).
Axes of the slice: x: 2, y: 2, z: 4, core: 2. Of those that a mesh axis runs over, the one named last changes fastest.
Arguments:
- weights: bfloat16 [16, 64, 64, 128], P('slab', 'dom'), may hold values from 0 to 0.049804688
- moments: bfloat16 [16, 64, 10, 128], P('slab', 'dom'), may hold values from -6 to 6
- block_tile: int32 [16, 64], P('slab', 'dom'), may hold values from 0 to 63, as said below
- block_slab: int32 [16, 64], P('slab', 'dom'), may hold values from 0 to 15, as said below
- block_count: int32 [16, 2], P('slab', 'dom'), may hold values from 8 to 32, as said below
Outputs:
- filtered: float32 [10, 32, 16, 128], P(None, 'slab', 'dom')
The draws below stay inside these ranges and needn't reach their ends.
Inputs may be any that keep to these rules, and one draw needn't show every extreme that they name: Every device's used blocks are its first block_count slots; in every slab one device uses all 32 slots. `block_slab`: A block's target slab is its own slab or one of the two next to it on the periodic loop. `block_tile`: A block whose target is the next slab names a tile of that slab's first plane (tiles below 32); one whose target is the previous slab a tile of that slab's last plane (tiles from 32).
All inputs are finite; a program needn't handle non-finite values.
Results may differ from the reference program's by a relative error of at most 0.00035.
Values may be sent and summed in bfloat16 or wider, within the bound.
A program may use at most 64 MiB of HBM per device.

```python
import jax
import jax.numpy as jnp
from jax import lax

MOM = 10
PB = 128
TC = 64
SX = 2
NZ = 128
BLK_DEV = 32
NY = 16
NX = 32
PT = 32
TILES = 64
BLOCKS = 64
N_DOM = 2
N_SLAB = 16


def routing_tables(key):
    base = jax.random.fold_in(key, 7)
    shape = (N_SLAB, N_DOM * BLK_DEV)
    kinds = jax.random.randint(jax.random.fold_in(base, 11), shape, 0, 4)
    column = jnp.arange(N_DOM * BLK_DEV, dtype=jnp.int32)[None, :]
    offset = jnp.where(kinds == 0, -1, jnp.where(kinds == 1, 1, 0))
    offset = jnp.where(column < 2, 0, offset)
    inner = jax.random.randint(jax.random.fold_in(base, 12), shape, 0, TILES)
    facing = jax.random.randint(jax.random.fold_in(base, 13), shape, 0, PT)
    tiles = jnp.where(offset == 0, inner, jnp.where(offset == 1, facing, (SX - 1) * PT + facing))
    tiles = jnp.where(column == 0, TILES - 1, jnp.where(column == 1, 0, tiles))
    slabs = jnp.mod(jnp.arange(N_SLAB, dtype=jnp.int32)[:, None] + offset, N_SLAB)
    return (tiles.astype(jnp.int32), slabs.astype(jnp.int32))


def draw_block_tile(key, part):
    return routing_tables(key)[0]


def draw_block_slab(key, part):
    return routing_tables(key)[1]


def draw_block_count(key, part):
    base = jax.random.fold_in(key, 29)
    counts = jax.random.randint(jax.random.fold_in(base, 1), (N_SLAB, N_DOM), max(1, BLK_DEV // 4), BLK_DEV // 2 + 1)
    fullest = jax.random.randint(jax.random.fold_in(base, 2), (N_SLAB, 1), 0, N_DOM)
    column = jnp.arange(N_DOM, dtype=jnp.int32)[None, :]
    return jnp.where(column == fullest, BLK_DEV, counts).astype(jnp.int32)


def level_of(own_key, shape, shards, low, top_value):
    def one(axis_at, blocks):
        heights = jax.random.uniform(jax.random.fold_in(jax.random.fold_in(own_key, 6), axis_at), (blocks,), jnp.float32, low / len(shards), top_value / len(shards))
        return jnp.repeat(jnp.exp(heights), shape[axis_at] // blocks).reshape((-1,) + (1,) * (len(shape) - axis_at - 1))

    gain = one(*shards[0])
    for cut in shards[1:]:
        gain = gain * one(*cut)
    return gain


def centred(own_key, dims, spread, limit, shards=(), held_as=jnp.bfloat16):
    array = spread * jax.random.normal(own_key, dims, jnp.float32)
    if shards:
        array = array * level_of(own_key, dims, shards, -0.22, 0.18)
    return jnp.clip(array, -limit, limit).astype(held_as)


def setup_inputs(seed: int = 0) -> dict:
    keys = jax.random.split(jax.random.key(seed), 6)
    return {
        "weights": jnp.clip(0.049804688 * jax.random.uniform(keys[0], (N_SLAB, BLOCKS, TC, PB), jnp.float32) ** level_of(keys[0], (N_SLAB, BLOCKS, TC, PB), ((0, 16), (1, 2)), -0.2, 0.2), 0.0, 0.049804688).astype(jnp.bfloat16),
        "moments": centred(keys[1], (N_SLAB, BLOCKS, MOM, PB), 1.0, 6.0, ((0, 16), (1, 2))),
        "block_tile": draw_block_tile(jax.random.fold_in(keys[5], 71), 0),
        "block_slab": draw_block_slab(jax.random.fold_in(keys[5], 71), 0),
        "block_count": draw_block_count(jax.random.fold_in(keys[5], 71), 0),
    }


def smooth_pass(field):
    adjacent_cell = jnp.roll(field, 1, axis=1) + jnp.roll(field, -1, axis=1)
    padded = jnp.pad(field, ((0, 0), (0, 0), (1, 1), (1, 1)))
    adjacent_cell = adjacent_cell + padded[:, :, 2:, 1:-1] + padded[:, :, :-2, 1:-1]
    adjacent_cell = adjacent_cell + padded[:, :, 1:-1, 2:] + padded[:, :, 1:-1, :-2]
    return field + 0.16 * (adjacent_cell - 6.0 * field)


def reference(weights, moments, block_tile, block_slab, block_count):
    slots = jnp.arange(BLOCKS, dtype=jnp.int32)
    slot_in_dev = slots % BLK_DEV
    device_of = slots // BLK_DEV

    def deposit_moments(grid, inputs):
        weight_blk, moment_blk, tile_blk, slab_blk, count_blk = inputs
        term_list = jnp.einsum("bmp,bcp->bmc", moment_blk.astype(jnp.float32), weight_blk.astype(jnp.float32))
        valid = (slot_in_dev < count_blk[device_of]).astype(jnp.float32)
        term_list = term_list * valid[:, None, None]
        target = (slab_blk * TILES + tile_blk).astype(jnp.int32)
        grid = grid.at[target].add(term_list.reshape(BLOCKS, MOM * TC))
        return grid, None

    start_grid = jnp.zeros((N_SLAB * TILES, MOM * TC), jnp.float32)
    grid, _ = lax.scan(deposit_moments, start_grid, (weights, moments, block_tile, block_slab, block_count))
    field = grid.reshape(NX, NY, NZ // TC, MOM, TC).transpose(3, 0, 1, 2, 4).reshape(MOM, NX, NY, NZ)
    field = smooth_pass(field)
    return smooth_pass(field)
```

```python
import functools

import jax
import jax.numpy as jnp
from jax import lax
from jax.experimental import pallas as pl
from jax.experimental.pallas import tpu as pltpu
from jax.sharding import PartitionSpec as P

SX = 2
RY = 8
NZ = 128
SUB = 16
PLANES = 8
diffusion = 0.16
MESH = pl.DeviceIdType.MESH
RANGES = {-2: (0, 1), -1: (1, 3), 0: (3, 5), 1: (5, 7), 2: (7, 8)}
ORDER = (2, -2, 1, -1, 0)


def in_plane(field, rows):
    count = field.shape[0]
    row = lax.broadcasted_iota(jnp.int32, field.shape, 0) % rows
    lane = lax.broadcasted_iota(jnp.int32, field.shape, 1)
    below = jnp.where(row == 0, 0.0, pltpu.roll(field, 1, 0))
    above = jnp.where(row == rows - 1, 0.0, pltpu.roll(field, count - 1, 0))
    left = jnp.where(lane == 0, 0.0, pltpu.roll(field, 1, 1))
    right = jnp.where(lane == NZ - 1, 0.0, pltpu.roll(field, NZ - 1, 1))
    near = (below + above) + (left + right)
    return (1.0 - 6.0 * diffusion) * field + diffusion * near


def two_passes(field, rows):
    once = in_plane(field, rows)
    twice = in_plane(once, rows) + (2.0 * diffusion * diffusion) * field
    planes = []
    for j in range(PLANES):
        e = j - 2
        total = None
        for source, at, factor in (
            (twice, e, 1.0),
            (once, e - 1, 2.0 * diffusion),
            (once, e + 1, 2.0 * diffusion),
            (field, e - 2, diffusion * diffusion),
            (field, e + 2, diffusion * diffusion),
        ):
            if 0 <= at < SX + 2:
                part = factor * source[at * rows : (at + 1) * rows]
                total = part if total is None else total + part
        planes.append(total)
    return planes


def kernel(
    n_doms, n_slabs,
    w_hbm, m_hbm, tile_hbm, slab_hbm, count_hbm, out_ref,
    w_ref, m_ref, tile_ref, slab_ref, count_ref,
    mpad, terms, sbuf, rbuf, load_sem, send_sem, recv_sem,
):
    my_dom = lax.axis_index("dom")
    my_slab = lax.axis_index("slab")
    loads = [
        pltpu.make_async_copy(src, dst, load_sem.at[i])
        for i, (src, dst) in enumerate(
            (
                (m_hbm.at[0], m_ref),
                (w_hbm.at[0], w_ref),
                (tile_hbm, tile_ref),
                (slab_hbm, slab_ref),
                (count_hbm, count_ref),
            )
        )
    ]
    for load in loads:
        load.start()

    peers = [(k, ds) for k in range(n_doms) for ds in ORDER if k or ds]

    def peer(k, ds):
        return (lax.rem(my_dom + k, n_doms), lax.rem(my_slab + ds + n_slabs, n_slabs))

    barrier = pltpu.get_barrier_semaphore()
    for k, ds in peers:
        pl.semaphore_signal(barrier, inc=1, device_id=peer(k, ds), device_id_type=MESH)

    mpad[...] = jnp.zeros_like(mpad)
    for load in loads:
        load.wait()
    blocks, moments, particles = m_ref.shape
    cells = w_ref.shape[1]
    rows = RY * n_doms
    plane_tiles = rows * (NZ // cells)
    half_rows = (SX + 2) * rows
    mpad[:, 0:moments, :] = m_ref[...]

    lane = lax.broadcasted_iota(jnp.int32, (SUB, NZ), 1)
    for j in range(blocks // 4):
        left = mpad[4 * j : 4 * j + 4].reshape(4 * SUB, particles)
        right = w_ref[4 * j : 4 * j + 4].reshape(4 * cells, particles)
        product = lax.dot_general(
            left, right, (((1,), (1,)), ((), ())), preferred_element_type=jnp.float32
        )
        for i in range(4):
            piece = product[SUB * i : SUB * (i + 1), NZ * (i // 2) : NZ * (i // 2 + 1)]
            other = pltpu.roll(piece, NZ // 2, 1)
            low, high = (piece, other) if i % 2 == 0 else (other, piece)
            b = 4 * j + i
            terms[SUB * b : SUB * (b + 1), :] = jnp.where(lane < cells, low, high)

    tile = tile_ref[...]
    step = slab_ref[...] - my_slab
    ahead = jnp.logical_or(step == 1, step == 1 - n_slabs)
    behind = jnp.logical_or(step == -1, step == n_slabs - 1)
    shift = jnp.where(ahead, SX + 1, jnp.where(behind, 1 - SX, 1)) * plane_tiles
    ext = tile + shift
    ext = (ext & 1) * half_rows + (ext >> 1)
    slot = lax.broadcasted_iota(jnp.int32, ext.shape, 1)
    ext = jnp.where(slot < count_ref[...], ext, -1)
    place = lax.broadcasted_iota(jnp.int32, (2 * half_rows, blocks), 0)
    hot = jnp.where(place == ext, 1.0, 0.0).astype(jnp.bfloat16)

    wide = lax.broadcasted_iota(jnp.int32, (half_rows, NZ), 1) < cells
    for m in range(moments):
        term = terms[pl.ds(m, blocks, stride=SUB), :]
        total = None
        for _ in range(3):
            part = term.astype(jnp.bfloat16)
            term = term - part.astype(jnp.float32)
            added = jnp.dot(hot, part, preferred_element_type=jnp.float32)
            total = added if total is None else total + added
        field = jnp.where(wide, total[:half_rows], total[half_rows:])
        planes = two_passes(field, rows)
        for j in range(PLANES):
            for d in range(n_doms):
                sbuf[d, j, m] = planes[j][RY * d : RY * (d + 1)]

    pl.semaphore_wait(barrier, len(peers))
    copies = []
    for n, (k, ds) in enumerate(peers):
        first, last = RANGES[ds]
        target = peer(k, ds)
        copies.append(
            pltpu.make_async_remote_copy(
                src_ref=sbuf.at[target[0], pl.ds(first, last - first)],
                dst_ref=rbuf.at[k, pl.ds(first, last - first)],
                send_sem=send_sem.at[n],
                recv_sem=recv_sem.at[n],
                device_id=target,
                device_id_type=MESH,
            )
        )
    for copy in copies:
        copy.start()
    own = sbuf.at[my_dom]
    even, odd = own[3], own[4]
    for (k, ds), copy in reversed(list(zip(peers, copies))):
        copy.wait_recv()
        first, last = RANGES[ds]
        for j in range(first, last):
            if j % 2:
                even = even + rbuf[k, j]
            else:
                odd = odd + rbuf[k, j]
    out_ref[:, 0] = even
    out_ref[:, 1] = odd
    for copy in copies:
        copy.wait_send()


def local(n_doms, n_slabs, weights, moments, block_tile, block_slab, block_count):
    _, blocks, cells, particles = weights.shape
    mom = moments.shape[2]
    n_peers = 5 * n_doms - 1
    return pl.pallas_call(
        functools.partial(kernel, n_doms, n_slabs),
        out_shape=jax.ShapeDtypeStruct((mom, SX, RY, NZ), jnp.float32),
        in_specs=[pl.BlockSpec(memory_space=pl.ANY)] * 5,
        out_specs=pl.BlockSpec(memory_space=pltpu.VMEM),
        scratch_shapes=[
            pltpu.VMEM((blocks, cells, particles), jnp.bfloat16),
            pltpu.VMEM((blocks, mom, particles), jnp.bfloat16),
            pltpu.VMEM((1, blocks), jnp.int32),
            pltpu.VMEM((1, blocks), jnp.int32),
            pltpu.VMEM((1, 1), jnp.int32),
            pltpu.VMEM((blocks, SUB, particles), jnp.bfloat16),
            pltpu.VMEM((blocks * SUB, NZ), jnp.float32),
            pltpu.VMEM((n_doms, PLANES, mom, RY, NZ), jnp.float32),
            pltpu.VMEM((n_doms, PLANES, mom, RY, NZ), jnp.float32),
            pltpu.SemaphoreType.DMA((5,)),
            pltpu.SemaphoreType.DMA((n_peers,)),
            pltpu.SemaphoreType.DMA((n_peers,)),
        ],
        compiler_params=pltpu.CompilerParams(
            collective_id=0, has_side_effects=True, vmem_limit_bytes=32 * 1024 * 1024
        ),
    )(weights, moments, block_tile, block_slab, block_count)


def solution(mesh):
    return jax.shard_map(
        functools.partial(local, mesh.shape["dom"], mesh.shape["slab"]),
        mesh=mesh,
        in_specs=(
            P("slab", "dom", None, None),
            P("slab", "dom", None, None),
            P("slab", "dom"),
            P("slab", "dom"),
            P("slab", "dom"),
        ),
        out_specs=P(None, "slab", "dom", None),
        check_vma=False,
    )
```

```python
import functools

import jax
import jax.numpy as jnp
from jax import lax
from jax.experimental import pallas as pl
from jax.experimental.pallas import tpu as pltpu
from jax.sharding import PartitionSpec as P

SX = 2
RY = 8
NZ = 128
SUB = 16
PLANES = 8
diffusion = 0.16
MESH = pl.DeviceIdType.MESH
RANGES = {-2: (0, 1), -1: (1, 3), 0: (3, 5), 1: (5, 7), 2: (7, 8)}
ORDER = (2, -2, 1, -1, 0)


def in_plane(field, rows):
    count = field.shape[0]
    row = lax.broadcasted_iota(jnp.int32, field.shape, 0) % rows
    lane = lax.broadcasted_iota(jnp.int32, field.shape, 1)
    below = jnp.where(row == 0, 0.0, pltpu.roll(field, 1, 0))
    above = jnp.where(row == rows - 1, 0.0, pltpu.roll(field, count - 1, 0))
    left = jnp.where(lane == 0, 0.0, pltpu.roll(field, 1, 1))
    right = jnp.where(lane == NZ - 1, 0.0, pltpu.roll(field, NZ - 1, 1))
    near = (below + above) + (left + right)
    return (1.0 - 6.0 * diffusion) * field + diffusion * near


def two_passes(field, rows):
    once = in_plane(field, rows)
    twice = in_plane(once, rows) + (2.0 * diffusion * diffusion) * field
    planes = []
    for j in range(PLANES):
        e = j - 2
        total = None
        for source, at, factor in (
            (twice, e, 1.0),
            (once, e - 1, 2.0 * diffusion),
            (once, e + 1, 2.0 * diffusion),
            (field, e - 2, diffusion * diffusion),
            (field, e + 2, diffusion * diffusion),
        ):
            if 0 <= at < SX + 2:
                part = factor * source[at * rows : (at + 1) * rows]
                total = part if total is None else total + part
        planes.append(total)
    return planes


def kernel(
    n_doms, n_slabs,
    w_hbm, m_hbm, tile_hbm, slab_hbm, count_hbm, out_ref,
    w_ref, m_ref, tile_ref, slab_ref, count_ref,
    terms, sbuf, rbuf, load_sem, send_sem, recv_sem,
):
    my_dom = lax.axis_index("dom")
    my_slab = lax.axis_index("slab")
    loads = [
        pltpu.make_async_copy(src, dst, load_sem.at[i])
        for i, (src, dst) in enumerate(
            (
                (m_hbm.at[0], m_ref),
                (w_hbm.at[0], w_ref),
                (tile_hbm, tile_ref),
                (slab_hbm, slab_ref),
                (count_hbm, count_ref),
            )
        )
    ]
    for load in loads:
        load.start()

    peers = [(k, ds) for k in range(n_doms) for ds in ORDER if k or ds]

    def peer(k, ds):
        return (lax.rem(my_dom + k, n_doms), lax.rem(my_slab + ds + n_slabs, n_slabs))

    barrier = pltpu.get_barrier_semaphore()
    for k, ds in peers:
        pl.semaphore_signal(barrier, inc=1, device_id=peer(k, ds), device_id_type=MESH)

    for load in loads:
        load.wait()
    moments, blocks, particles = m_ref.shape
    cells = w_ref.shape[1]
    rows = RY * n_doms
    plane_tiles = rows * (NZ // cells)
    half_rows = (SX + 2) * rows

    row = lax.broadcasted_iota(jnp.int32, (8, NZ), 0)
    lane = lax.broadcasted_iota(jnp.int32, (8, NZ), 1)
    in_place = (row % 2 == 0) == (lane < cells)
    for g in range(blocks // SUB):
        left = m_ref[:, SUB * g : SUB * (g + 1), :].reshape(moments * SUB, particles)
        right = w_ref[SUB * g : SUB * (g + 1)].reshape(SUB * cells, particles)
        product = lax.dot_general(
            left, right, (((1,), (1,)), ((), ())), preferred_element_type=jnp.float32
        )
        for m in range(moments):
            for h in range(2):
                top = SUB * m + 8 * h
                piece = None
                for pair in range(4):
                    at = NZ * (4 * h + pair)
                    found = product[top : top + 8, at : at + NZ]
                    piece = found if piece is None else jnp.where(row // 2 == pair, found, piece)
                both = jnp.where(in_place, piece, pltpu.roll(piece, NZ // 2, 1))
                terms[m, SUB * g + 8 * h : SUB * g + 8 * (h + 1), :] = both

    tile = tile_ref[...]
    step = slab_ref[...] - my_slab
    ahead = jnp.logical_or(step == 1, step == 1 - n_slabs)
    behind = jnp.logical_or(step == -1, step == n_slabs - 1)
    shift = jnp.where(ahead, SX + 1, jnp.where(behind, 1 - SX, 1)) * plane_tiles
    ext = tile + shift
    ext = (ext & 1) * half_rows + (ext >> 1)
    slot = lax.broadcasted_iota(jnp.int32, ext.shape, 1)
    ext = jnp.where(slot < count_ref[...], ext, -1)
    place = lax.broadcasted_iota(jnp.int32, (2 * half_rows, blocks), 0)
    hot = jnp.where(place == ext, 1.0, 0.0).astype(jnp.bfloat16)

    wide = lax.broadcasted_iota(jnp.int32, (half_rows, NZ), 1) < cells
    for m in range(moments):
        term = terms[m]
        total = None
        for _ in range(3):
            part = term.astype(jnp.bfloat16)
            term = term - part.astype(jnp.float32)
            added = jnp.dot(hot, part, preferred_element_type=jnp.float32)
            total = added if total is None else total + added
        field = jnp.where(wide, total[:half_rows], total[half_rows:])
        planes = two_passes(field, rows)
        for j in range(PLANES):
            for d in range(n_doms):
                sbuf[d, j, m] = planes[j][RY * d : RY * (d + 1)]

    pl.semaphore_wait(barrier, len(peers))
    copies = []
    for n, (k, ds) in enumerate(peers):
        first, last = RANGES[ds]
        target = peer(k, ds)
        copies.append(
            pltpu.make_async_remote_copy(
                src_ref=sbuf.at[target[0], pl.ds(first, last - first)],
                dst_ref=rbuf.at[k, pl.ds(first, last - first)],
                send_sem=send_sem.at[n],
                recv_sem=recv_sem.at[n],
                device_id=target,
                device_id_type=MESH,
            )
        )
    for copy in copies:
        copy.start()
    own = sbuf.at[my_dom]
    even, odd = own[3], own[4]
    for (k, ds), copy in reversed(list(zip(peers, copies))):
        copy.wait_recv()
        first, last = RANGES[ds]
        for j in range(first, last):
            if j % 2:
                even = even + rbuf[k, j]
            else:
                odd = odd + rbuf[k, j]
    out_ref[:, 0] = even
    out_ref[:, 1] = odd
    for copy in copies:
        copy.wait_send()


def local(n_doms, n_slabs, weights, moments, block_tile, block_slab, block_count):
    _, blocks, cells, particles = weights.shape
    mom = moments.shape[2]
    n_peers = 5 * n_doms - 1
    return pl.pallas_call(
        functools.partial(kernel, n_doms, n_slabs),
        out_shape=jax.ShapeDtypeStruct((mom, SX, RY, NZ), jnp.float32),
        in_specs=[pl.BlockSpec(memory_space=pl.ANY)] * 5,
        out_specs=pl.BlockSpec(memory_space=pltpu.VMEM),
        scratch_shapes=[
            pltpu.VMEM((blocks, cells, particles), jnp.bfloat16),
            pltpu.VMEM((mom, blocks, particles), jnp.bfloat16),
            pltpu.VMEM((1, blocks), jnp.int32),
            pltpu.VMEM((1, blocks), jnp.int32),
            pltpu.VMEM((1, 1), jnp.int32),
            pltpu.VMEM((mom, blocks, NZ), jnp.float32),
            pltpu.VMEM((n_doms, PLANES, mom, RY, NZ), jnp.float32),
            pltpu.VMEM((n_doms, PLANES, mom, RY, NZ), jnp.float32),
            pltpu.SemaphoreType.DMA((5,)),
            pltpu.SemaphoreType.DMA((n_peers,)),
            pltpu.SemaphoreType.DMA((n_peers,)),
        ],
        compiler_params=pltpu.CompilerParams(
            collective_id=0, has_side_effects=True, vmem_limit_bytes=64 * 1024 * 1024
        ),
    )(weights, moments.transpose(0, 2, 1, 3), block_tile, block_slab, block_count)


def solution(mesh):
    return jax.shard_map(
        functools.partial(local, mesh.shape["dom"], mesh.shape["slab"]),
        mesh=mesh,
        in_specs=(
            P("slab", "dom", None, None),
            P("slab", "dom", None, None),
            P("slab", "dom"),
            P("slab", "dom"),
            P("slab", "dom"),
        ),
        out_specs=P(None, "slab", "dom", None),
        check_vma=False,
    )
```

```python
import functools

import jax
import jax.numpy as jnp
from jax import lax
from jax.experimental import pallas as pl
from jax.experimental.pallas import tpu as pltpu
from jax.sharding import PartitionSpec as P

SX = 2
RY = 8
NZ = 128
SUB = 16
PLANES = 8
LEVELS = 32766.0
SMALLEST = 1e-33
diffusion = 0.16
MESH = pl.DeviceIdType.MESH
RANGES = {-2: (0, 1), -1: (1, 3), 0: (3, 5), 1: (5, 7), 2: (7, 8)}
ORDER = (2, -2, 1, -1, 0)


def in_plane(field, rows):
    count = field.shape[0]
    row = lax.broadcasted_iota(jnp.int32, field.shape, 0) % rows
    lane = lax.broadcasted_iota(jnp.int32, field.shape, 1)
    below = jnp.where(row == 0, 0.0, pltpu.roll(field, 1, 0))
    above = jnp.where(row == rows - 1, 0.0, pltpu.roll(field, count - 1, 0))
    left = jnp.where(lane == 0, 0.0, pltpu.roll(field, 1, 1))
    right = jnp.where(lane == NZ - 1, 0.0, pltpu.roll(field, NZ - 1, 1))
    near = (below + above) + (left + right)
    return (1.0 - 6.0 * diffusion) * field + diffusion * near


def two_passes(field, rows):
    once = in_plane(field, rows)
    twice = in_plane(once, rows) + (2.0 * diffusion * diffusion) * field
    planes = []
    for j in range(PLANES):
        e = j - 2
        total = None
        for source, at, factor in (
            (twice, e, 1.0),
            (once, e - 1, 2.0 * diffusion),
            (once, e + 1, 2.0 * diffusion),
            (field, e - 2, diffusion * diffusion),
            (field, e + 2, diffusion * diffusion),
        ):
            if 0 <= at < SX + 2:
                part = factor * source[at * rows : (at + 1) * rows]
                total = part if total is None else total + part
        planes.append(total)
    return planes


def kernel(
    n_doms, n_slabs,
    w_hbm, m_hbm, tile_hbm, slab_hbm, count_hbm, out_ref,
    w_ref, m_ref, tile_ref, slab_ref, count_ref,
    terms, fields, peaks, send_scale, send_level, recv_scale, recv_level,
    load_sem, send_sem, recv_sem,
):
    my_dom = lax.axis_index("dom")
    my_slab = lax.axis_index("slab")
    loads = [
        pltpu.make_async_copy(src, dst, load_sem.at[i])
        for i, (src, dst) in enumerate(
            (
                (m_hbm.at[0], m_ref),
                (w_hbm.at[0], w_ref),
                (tile_hbm, tile_ref),
                (slab_hbm, slab_ref),
                (count_hbm, count_ref),
            )
        )
    ]
    for load in loads:
        load.start()

    peers = [(k, ds) for k in range(n_doms) for ds in ORDER if k or ds]

    def peer(k, ds):
        return (lax.rem(my_dom + k, n_doms), lax.rem(my_slab + ds + n_slabs, n_slabs))

    barrier = pltpu.get_barrier_semaphore()
    for k, ds in peers:
        pl.semaphore_signal(barrier, inc=1, device_id=peer(k, ds), device_id_type=MESH)

    for load in loads:
        load.wait()
    moments, blocks, particles = m_ref.shape
    cells = w_ref.shape[1]
    rows = RY * n_doms
    plane_tiles = rows * (NZ // cells)
    half_rows = (SX + 2) * rows

    row = lax.broadcasted_iota(jnp.int32, (8, NZ), 0)
    lane = lax.broadcasted_iota(jnp.int32, (8, NZ), 1)
    in_place = (row % 2 == 0) == (lane < cells)
    for g in range(blocks // SUB):
        left = m_ref[:, SUB * g : SUB * (g + 1), :].reshape(moments * SUB, particles)
        right = w_ref[SUB * g : SUB * (g + 1)].reshape(SUB * cells, particles)
        product = lax.dot_general(
            left, right, (((1,), (1,)), ((), ())), preferred_element_type=jnp.float32
        )
        for m in range(moments):
            for h in range(2):
                top = SUB * m + 8 * h
                piece = None
                for pair in range(4):
                    at = NZ * (4 * h + pair)
                    found = product[top : top + 8, at : at + NZ]
                    piece = found if piece is None else jnp.where(row // 2 == pair, found, piece)
                both = jnp.where(in_place, piece, pltpu.roll(piece, NZ // 2, 1))
                terms[m, SUB * g + 8 * h : SUB * g + 8 * (h + 1), :] = both

    tile = tile_ref[...]
    step = slab_ref[...] - my_slab
    ahead = jnp.logical_or(step == 1, step == 1 - n_slabs)
    behind = jnp.logical_or(step == -1, step == n_slabs - 1)
    shift = jnp.where(ahead, SX + 1, jnp.where(behind, 1 - SX, 1)) * plane_tiles
    ext = tile + shift
    ext = (ext & 1) * half_rows + (ext >> 1)
    slot = lax.broadcasted_iota(jnp.int32, ext.shape, 1)
    ext = jnp.where(slot < count_ref[...], ext, -1)
    place = lax.broadcasted_iota(jnp.int32, (2 * half_rows, blocks), 0)
    hot = jnp.where(place == ext, 1.0, 0.0).astype(jnp.bfloat16)

    wide = lax.broadcasted_iota(jnp.int32, (half_rows, NZ), 1) < cells
    for m in range(moments):
        term = terms[m]
        total = None
        for _ in range(3):
            part = term.astype(jnp.bfloat16)
            term = term - part.astype(jnp.float32)
            added = jnp.dot(hot, part, preferred_element_type=jnp.float32)
            total = added if total is None else total + added
        field = jnp.where(wide, total[:half_rows], total[half_rows:])
        planes = two_passes(field, rows)
        for j in range(PLANES):
            for d in range(n_doms):
                block = planes[j][RY * d : RY * (d + 1)]
                fields[d, j, m] = block
                peak = jnp.abs(block)
                peaks[d, j] = peak if m == 0 else jnp.maximum(peaks[d, j], peak)

    copies = []
    for n, ds in enumerate(ORDER):
        first, last = RANGES[ds]
        for d in range(n_doms):
            for j in range(first, last):
                peak = jnp.maximum(jnp.max(peaks[d, j], axis=0, keepdims=True), SMALLEST)
                send_scale[d, j] = peak * (1.0 / LEVELS)
                inverse = LEVELS / peak
                for p in range(moments // 2):
                    pair = fields[d, j, 2 * p : 2 * p + 2].reshape(2 * RY, NZ)
                    level = jnp.round(pair * inverse).astype(jnp.int32)
                    send_level[d, j, p] = level.astype(jnp.int16)
        if n == 0:
            pl.semaphore_wait(barrier, len(peers))
        span = pl.ds(first, last - first)
        for k in range(n_doms):
            if k == 0 and ds == 0:
                continue
            target = peer(k, ds)
            group = []
            for i, (source, landing) in enumerate(
                ((send_scale, recv_scale), (send_level, recv_level))
            ):
                copy = pltpu.make_async_remote_copy(
                    src_ref=source.at[target[0], span],
                    dst_ref=landing.at[k, span],
                    send_sem=send_sem.at[i, k, n],
                    recv_sem=recv_sem.at[i, k, n],
                    device_id=target,
                    device_id_type=MESH,
                )
                copy.start()
                group.append(copy)
            copies.append((k, ds, group))

    own = fields.at[my_dom]
    sums = [own[4], own[3]]
    for k, ds, group in reversed(copies):
        for copy in group:
            copy.wait_recv()
        for j in range(*RANGES[ds]):
            level = recv_level[k, j].astype(jnp.float32).reshape(moments, RY, NZ)
            sums[j % 2] = sums[j % 2] + level * recv_scale[k, j]
    out_ref[:, 0] = sums[1]
    out_ref[:, 1] = sums[0]
    for _, _, group in copies:
        for copy in group:
            copy.wait_send()


def local(n_doms, n_slabs, weights, moments, block_tile, block_slab, block_count):
    _, blocks, cells, particles = weights.shape
    mom = moments.shape[2]
    return pl.pallas_call(
        functools.partial(kernel, n_doms, n_slabs),
        out_shape=jax.ShapeDtypeStruct((mom, SX, RY, NZ), jnp.float32),
        in_specs=[pl.BlockSpec(memory_space=pl.ANY)] * 5,
        out_specs=pl.BlockSpec(memory_space=pltpu.VMEM),
        scratch_shapes=[
            pltpu.VMEM((blocks, cells, particles), jnp.bfloat16),
            pltpu.VMEM((mom, blocks, particles), jnp.bfloat16),
            pltpu.VMEM((1, blocks), jnp.int32),
            pltpu.VMEM((1, blocks), jnp.int32),
            pltpu.VMEM((1, 1), jnp.int32),
            pltpu.VMEM((mom, blocks, NZ), jnp.float32),
            pltpu.VMEM((n_doms, PLANES, mom, RY, NZ), jnp.float32),
            pltpu.VMEM((n_doms, PLANES, RY, NZ), jnp.float32),
            pltpu.VMEM((n_doms, PLANES, 1, NZ), jnp.float32),
            pltpu.VMEM((n_doms, PLANES, mom // 2, 2 * RY, NZ), jnp.int16),
            pltpu.VMEM((n_doms, PLANES, 1, NZ), jnp.float32),
            pltpu.VMEM((n_doms, PLANES, mom // 2, 2 * RY, NZ), jnp.int16),
            pltpu.SemaphoreType.DMA((5,)),
            pltpu.SemaphoreType.DMA((2, n_doms, len(ORDER))),
            pltpu.SemaphoreType.DMA((2, n_doms, len(ORDER))),
        ],
        compiler_params=pltpu.CompilerParams(
            collective_id=0, has_side_effects=True, vmem_limit_bytes=64 * 1024 * 1024
        ),
    )(weights, moments.transpose(0, 2, 1, 3), block_tile, block_slab, block_count)


def solution(mesh):
    return jax.shard_map(
        functools.partial(local, mesh.shape["dom"], mesh.shape["slab"]),
        mesh=mesh,
        in_specs=(
            P("slab", "dom", None, None),
            P("slab", "dom", None, None),
            P("slab", "dom"),
            P("slab", "dom"),
            P("slab", "dom"),
        ),
        out_specs=P(None, "slab", "dom", None),
        check_vma=False,
    )
```

```python
import functools

import jax
import jax.numpy as jnp
from jax import lax
from jax.experimental import pallas as pl
from jax.experimental.pallas import tpu as pltpu
from jax.sharding import PartitionSpec as P

SX = 2
RY = 8
NZ = 128
SUB = 16
PLANES = 8
LOADS = 4
LEVELS = 32766.0
SMALLEST = 1e-33
diffusion = 0.16
MESH = pl.DeviceIdType.MESH
RANGES = {-2: (0, 1), -1: (1, 3), 0: (3, 5), 1: (5, 7), 2: (7, 8)}
ORDER = (2, -2, 1, -1, 0)


def in_plane(field, rows):
    count = field.shape[0]
    row = lax.broadcasted_iota(jnp.int32, field.shape, 0) % rows
    lane = lax.broadcasted_iota(jnp.int32, field.shape, 1)
    below = jnp.where(row == 0, 0.0, pltpu.roll(field, 1, 0))
    above = jnp.where(row == rows - 1, 0.0, pltpu.roll(field, count - 1, 0))
    left = jnp.where(lane == 0, 0.0, pltpu.roll(field, 1, 1))
    right = jnp.where(lane == NZ - 1, 0.0, pltpu.roll(field, NZ - 1, 1))
    near = (below + above) + (left + right)
    return (1.0 - 6.0 * diffusion) * field + diffusion * near


def two_passes(field, rows):
    once = in_plane(field, rows)
    twice = in_plane(once, rows) + (2.0 * diffusion * diffusion) * field
    planes = []
    for j in range(PLANES):
        e = j - 2
        total = None
        for source, at, factor in (
            (twice, e, 1.0),
            (once, e - 1, 2.0 * diffusion),
            (once, e + 1, 2.0 * diffusion),
            (field, e - 2, diffusion * diffusion),
            (field, e + 2, diffusion * diffusion),
        ):
            if 0 <= at < SX + 2:
                part = factor * source[at * rows : (at + 1) * rows]
                total = part if total is None else total + part
        planes.append(total)
    return planes


def kernel(
    n_doms, n_slabs,
    w_hbm, m_hbm, tile_hbm, slab_hbm, count_hbm, out_ref,
    w_ref, m_ref, tile_ref, slab_ref, count_ref,
    terms, fields, peaks, send_scale, send_level, recv_scale, recv_level,
    load_sem, send_sem, recv_sem,
):
    my_dom = lax.axis_index("dom")
    my_slab = lax.axis_index("slab")
    moments, blocks, particles = m_ref.shape
    cells = w_ref.shape[1]
    pairs = [(tile_hbm, tile_ref), (slab_hbm, slab_ref), (count_hbm, count_ref), (m_hbm.at[0], m_ref)]
    for g in range(LOADS):
        part = pl.ds(g * (blocks // LOADS), blocks // LOADS)
        pairs.append((w_hbm.at[0, part], w_ref.at[part]))
    loads = [
        pltpu.make_async_copy(src, dst, load_sem.at[i]) for i, (src, dst) in enumerate(pairs)
    ]
    for load in loads:
        load.start()

    peers = [(k, ds) for k in range(n_doms) for ds in ORDER if k or ds]

    def peer(k, ds):
        return (lax.rem(my_dom + k, n_doms), lax.rem(my_slab + ds + n_slabs, n_slabs))

    barrier = pltpu.get_barrier_semaphore()
    for k, ds in peers:
        pl.semaphore_signal(barrier, inc=1, device_id=peer(k, ds), device_id_type=MESH)

    for load in loads[:3]:
        load.wait()
    rows = RY * n_doms
    plane_tiles = rows * (NZ // cells)
    half_rows = (SX + 2) * rows

    tile = tile_ref[...]
    step = slab_ref[...] - my_slab
    ahead = jnp.logical_or(step == 1, step == 1 - n_slabs)
    behind = jnp.logical_or(step == -1, step == n_slabs - 1)
    shift = jnp.where(ahead, SX + 1, jnp.where(behind, 1 - SX, 1)) * plane_tiles
    ext = tile + shift
    ext = (ext & 1) * half_rows + (ext >> 1)
    slot = lax.broadcasted_iota(jnp.int32, ext.shape, 1)
    ext = jnp.where(slot < count_ref[...], ext, -1)
    place = lax.broadcasted_iota(jnp.int32, (2 * half_rows, blocks), 0)
    hot = jnp.where(place == ext, 1.0, 0.0).astype(jnp.bfloat16)

    row = lax.broadcasted_iota(jnp.int32, (8, NZ), 0)
    lane = lax.broadcasted_iota(jnp.int32, (8, NZ), 1)
    in_place = (row % 2 == 0) == (lane < cells)
    loads[3].wait()
    for g in range(blocks // SUB):
        share = LOADS * SUB // blocks
        for load in loads[4 + share * g : 4 + share * (g + 1)]:
            load.wait()
        left = m_ref[:, SUB * g : SUB * (g + 1), :].reshape(moments * SUB, particles)
        right = w_ref[SUB * g : SUB * (g + 1)].reshape(SUB * cells, particles)
        product = lax.dot_general(
            left, right, (((1,), (1,)), ((), ())), preferred_element_type=jnp.float32
        )
        for m in range(moments):
            for h in range(2):
                top = SUB * m + 8 * h
                piece = None
                for pair in range(4):
                    at = NZ * (4 * h + pair)
                    found = product[top : top + 8, at : at + NZ]
                    piece = found if piece is None else jnp.where(row // 2 == pair, found, piece)
                both = jnp.where(in_place, piece, pltpu.roll(piece, NZ // 2, 1))
                terms[m, SUB * g + 8 * h : SUB * g + 8 * (h + 1), :] = both

    wide = lax.broadcasted_iota(jnp.int32, (half_rows, NZ), 1) < cells
    for m in range(moments):
        term = terms[m]
        total = None
        for _ in range(2):
            part = term.astype(jnp.bfloat16)
            term = term - part.astype(jnp.float32)
            added = jnp.dot(hot, part, preferred_element_type=jnp.float32)
            total = added if total is None else total + added
        field = jnp.where(wide, total[:half_rows], total[half_rows:])
        planes = two_passes(field, rows)
        for j in range(PLANES):
            for d in range(n_doms):
                block = planes[j][RY * d : RY * (d + 1)]
                fields[d, j, m] = block
                peak = jnp.abs(block)
                peaks[d, j] = peak if m == 0 else jnp.maximum(peaks[d, j], peak)

    copies = []
    for n, ds in enumerate(ORDER):
        first, last = RANGES[ds]
        for d in range(n_doms):
            for j in range(first, last):
                peak = jnp.maximum(jnp.max(peaks[d, j], axis=0, keepdims=True), SMALLEST)
                send_scale[d, j] = peak * (1.0 / LEVELS)
                inverse = LEVELS / peak
                for p in range(moments // 2):
                    pair = fields[d, j, 2 * p : 2 * p + 2].reshape(2 * RY, NZ)
                    level = jnp.round(pair * inverse).astype(jnp.int32)
                    send_level[d, j, p] = level.astype(jnp.int16)
        if n == 0:
            pl.semaphore_wait(barrier, len(peers))
        span = pl.ds(first, last - first)
        for k in range(n_doms):
            if k == 0 and ds == 0:
                continue
            target = peer(k, ds)
            group = []
            for i, (source, landing) in enumerate(
                ((send_scale, recv_scale), (send_level, recv_level))
            ):
                copy = pltpu.make_async_remote_copy(
                    src_ref=source.at[target[0], span],
                    dst_ref=landing.at[k, span],
                    send_sem=send_sem.at[i, k, n],
                    recv_sem=recv_sem.at[i, k, n],
                    device_id=target,
                    device_id_type=MESH,
                )
                copy.start()
                group.append(copy)
            copies.append((k, ds, group))

    own = fields.at[my_dom]
    sums = [own[4], own[3]]
    for k, ds, group in reversed(copies):
        for copy in group:
            copy.wait_recv()
        for j in range(*RANGES[ds]):
            level = recv_level[k, j].astype(jnp.float32).reshape(moments, RY, NZ)
            sums[j % 2] = sums[j % 2] + level * recv_scale[k, j]
    out_ref[:, 0] = sums[1]
    out_ref[:, 1] = sums[0]
    for _, _, group in copies:
        for copy in group:
            copy.wait_send()


def local(n_doms, n_slabs, weights, moments, block_tile, block_slab, block_count):
    _, blocks, cells, particles = weights.shape
    mom = moments.shape[2]
    return pl.pallas_call(
        functools.partial(kernel, n_doms, n_slabs),
        out_shape=jax.ShapeDtypeStruct((mom, SX, RY, NZ), jnp.float32),
        in_specs=[pl.BlockSpec(memory_space=pl.ANY)] * 5,
        out_specs=pl.BlockSpec(memory_space=pltpu.VMEM),
        scratch_shapes=[
            pltpu.VMEM((blocks, cells, particles), jnp.bfloat16),
            pltpu.VMEM((mom, blocks, particles), jnp.bfloat16),
            pltpu.VMEM((1, blocks), jnp.int32),
            pltpu.VMEM((1, blocks), jnp.int32),
            pltpu.VMEM((1, 1), jnp.int32),
            pltpu.VMEM((mom, blocks, NZ), jnp.float32),
            pltpu.VMEM((n_doms, PLANES, mom, RY, NZ), jnp.float32),
            pltpu.VMEM((n_doms, PLANES, RY, NZ), jnp.float32),
            pltpu.VMEM((n_doms, PLANES, 1, NZ), jnp.float32),
            pltpu.VMEM((n_doms, PLANES, mom // 2, 2 * RY, NZ), jnp.int16),
            pltpu.VMEM((n_doms, PLANES, 1, NZ), jnp.float32),
            pltpu.VMEM((n_doms, PLANES, mom // 2, 2 * RY, NZ), jnp.int16),
            pltpu.SemaphoreType.DMA((4 + LOADS,)),
            pltpu.SemaphoreType.DMA((2, n_doms, len(ORDER))),
            pltpu.SemaphoreType.DMA((2, n_doms, len(ORDER))),
        ],
        compiler_params=pltpu.CompilerParams(
            collective_id=0, has_side_effects=True, vmem_limit_bytes=64 * 1024 * 1024 - 10432 * 1024
        ),
    )(weights, moments.transpose(0, 2, 1, 3), block_tile, block_slab, block_count)


def solution(mesh):
    return jax.shard_map(
        functools.partial(local, mesh.shape["dom"], mesh.shape["slab"]),
        mesh=mesh,
        in_specs=(
            P("slab", "dom", None, None),
            P("slab", "dom", None, None),
            P("slab", "dom"),
            P("slab", "dom"),
            P("slab", "dom"),
        ),
        out_specs=P(None, "slab", "dom", None),
        check_vma=False,
    )
```

```python
import functools

import jax
import jax.numpy as jnp
from jax import lax
from jax.experimental import pallas as pl
from jax.experimental.pallas import tpu as pltpu
from jax.sharding import PartitionSpec as P

SX = 2
RY = 8
NZ = 128
SUB = 16
PLANES = 8
LOADS = 4
LEVELS = 32766.0
SMALLEST = 1e-33
diffusion = 0.16
MESH = pl.DeviceIdType.MESH
RANGES = {-2: (0, 1), -1: (1, 3), 0: (3, 5), 1: (5, 7), 2: (7, 8)}
ORDER = (2, -2, 1, -1, 0)


def in_plane(field, rows):
    count = field.shape[0]
    row = lax.broadcasted_iota(jnp.int32, field.shape, 0) % rows
    lane = lax.broadcasted_iota(jnp.int32, field.shape, 1)
    below = jnp.where(row == 0, 0.0, pltpu.roll(field, 1, 0))
    above = jnp.where(row == rows - 1, 0.0, pltpu.roll(field, count - 1, 0))
    left = jnp.where(lane == 0, 0.0, pltpu.roll(field, 1, 1))
    right = jnp.where(lane == NZ - 1, 0.0, pltpu.roll(field, NZ - 1, 1))
    near = (below + above) + (left + right)
    return (1.0 - 6.0 * diffusion) * field + diffusion * near


def two_passes(field, rows):
    once = in_plane(field, rows)
    twice = in_plane(once, rows) + (2.0 * diffusion * diffusion) * field
    planes = []
    for j in range(PLANES):
        e = j - 2
        total = None
        for source, at, factor in (
            (twice, e, 1.0),
            (once, e - 1, 2.0 * diffusion),
            (once, e + 1, 2.0 * diffusion),
            (field, e - 2, diffusion * diffusion),
            (field, e + 2, diffusion * diffusion),
        ):
            if 0 <= at < SX + 2:
                part = factor * source[at * rows : (at + 1) * rows]
                total = part if total is None else total + part
        planes.append(total)
    return planes


def kernel(
    n_doms, n_slabs,
    w_hbm, m_hbm, tile_hbm, slab_hbm, count_hbm, out_ref,
    w_ref, m_ref, tile_ref, slab_ref, count_ref,
    terms, fields, peaks, send_scale, send_level, recv_scale, recv_level,
    load_sem, send_sem, recv_sem,
):
    my_dom = lax.axis_index("dom")
    my_slab = lax.axis_index("slab")
    moments, blocks, particles = m_ref.shape
    cells = w_ref.shape[1]
    pairs = [(tile_hbm, tile_ref), (slab_hbm, slab_ref), (count_hbm, count_ref), (m_hbm.at[0], m_ref)]
    for g in range(LOADS):
        part = pl.ds(g * (blocks // LOADS), blocks // LOADS)
        pairs.append((w_hbm.at[0, part], w_ref.at[part]))
    loads = [
        pltpu.make_async_copy(src, dst, load_sem.at[i]) for i, (src, dst) in enumerate(pairs)
    ]
    for load in loads:
        load.start()

    peers = [(k, ds) for k in range(n_doms) for ds in ORDER if k or ds]

    def peer(k, ds):
        return (lax.rem(my_dom + k, n_doms), lax.rem(my_slab + ds + n_slabs, n_slabs))

    barrier = pltpu.get_barrier_semaphore()
    for k, ds in peers:
        pl.semaphore_signal(barrier, inc=1, device_id=peer(k, ds), device_id_type=MESH)

    for load in loads[:3]:
        load.wait()
    rows = RY * n_doms
    plane_tiles = rows * (NZ // cells)
    half_rows = (SX + 2) * rows

    tile = tile_ref[...]
    step = slab_ref[...] - my_slab
    ahead = jnp.logical_or(step == 1, step == 1 - n_slabs)
    behind = jnp.logical_or(step == -1, step == n_slabs - 1)
    shift = jnp.where(ahead, SX + 1, jnp.where(behind, 1 - SX, 1)) * plane_tiles
    ext = tile + shift
    ext = (ext & 1) * half_rows + (ext >> 1)
    slot = lax.broadcasted_iota(jnp.int32, ext.shape, 1)
    ext = jnp.where(slot < count_ref[...], ext, -1)
    place = lax.broadcasted_iota(jnp.int32, (2 * half_rows, blocks), 0)
    hot = jnp.where(place == ext, 1.0, 0.0).astype(jnp.bfloat16)

    row = lax.broadcasted_iota(jnp.int32, (8, NZ), 0)
    lane = lax.broadcasted_iota(jnp.int32, (8, NZ), 1)
    in_place = (row % 2 == 0) == (lane < cells)
    loads[3].wait()
    for g in range(blocks // SUB):
        share = LOADS * SUB // blocks
        for load in loads[4 + share * g : 4 + share * (g + 1)]:
            load.wait()
        left = m_ref[:, SUB * g : SUB * (g + 1), :].reshape(moments * SUB, particles)
        right = w_ref[SUB * g : SUB * (g + 1)].reshape(SUB * cells, particles)
        product = lax.dot_general(
            left, right, (((1,), (1,)), ((), ())), preferred_element_type=jnp.float32
        )
        for m in range(moments):
            for h in range(2):
                top = SUB * m + 8 * h
                piece = None
                for pair in range(4):
                    at = NZ * (4 * h + pair)
                    found = product[top : top + 8, at : at + NZ]
                    piece = found if piece is None else jnp.where(row // 2 == pair, found, piece)
                both = jnp.where(in_place, piece, pltpu.roll(piece, NZ // 2, 1))
                terms[m, SUB * g + 8 * h : SUB * g + 8 * (h + 1), :] = both

    wide = lax.broadcasted_iota(jnp.int32, (half_rows, NZ), 1) < cells
    for m in range(moments):
        term = terms[m]
        total = None
        for _ in range(2):
            part = term.astype(jnp.bfloat16)
            term = term - part.astype(jnp.float32)
            added = jnp.dot(hot, part, preferred_element_type=jnp.float32)
            total = added if total is None else total + added
        field = jnp.where(wide, total[:half_rows], total[half_rows:])
        planes = two_passes(field, rows)
        for j in range(PLANES):
            for d in range(n_doms):
                block = planes[j][RY * d : RY * (d + 1)]
                fields[d, j, m] = block
                peak = jnp.abs(block)
                peaks[d, j] = peak if m == 0 else jnp.maximum(peaks[d, j], peak)

    copies = []
    for n, ds in enumerate(ORDER):
        first, last = RANGES[ds]
        for d in range(n_doms):
            for j in range(first, last):
                peak = jnp.maximum(jnp.max(peaks[d, j], axis=0, keepdims=True), SMALLEST)
                send_scale[d, j] = peak * (1.0 / LEVELS)
                inverse = LEVELS / peak
                for p in range(moments // 2):
                    pair = fields[d, j, 2 * p : 2 * p + 2].reshape(2 * RY, NZ)
                    level = jnp.round(pair * inverse).astype(jnp.int32)
                    send_level[d, j, p] = level.astype(jnp.int16)
        if n == 0:
            pl.semaphore_wait(barrier, len(peers))
        span = pl.ds(first, last - first)
        for k in reversed(range(n_doms)):
            if k == 0 and ds == 0:
                continue
            target = peer(k, ds)
            group = []
            for i, (source, landing) in enumerate(
                ((send_scale, recv_scale), (send_level, recv_level))
            ):
                copy = pltpu.make_async_remote_copy(
                    src_ref=source.at[target[0], span],
                    dst_ref=landing.at[k, span],
                    send_sem=send_sem.at[i, k, n],
                    recv_sem=recv_sem.at[i, k, n],
                    device_id=target,
                    device_id_type=MESH,
                )
                copy.start()
                group.append(copy)
            copies.append((k, ds, group))

    own = fields.at[my_dom]
    sums = [own[4], own[3]]
    for k, ds, group in reversed(copies):
        for copy in group:
            copy.wait_recv()
        for j in range(*RANGES[ds]):
            level = recv_level[k, j].astype(jnp.float32).reshape(moments, RY, NZ)
            sums[j % 2] = sums[j % 2] + level * recv_scale[k, j]
    out_ref[:, 0] = sums[1]
    out_ref[:, 1] = sums[0]
    for _, _, group in copies:
        for copy in group:
            copy.wait_send()


def local(n_doms, n_slabs, weights, moments, block_tile, block_slab, block_count):
    _, blocks, cells, particles = weights.shape
    mom = moments.shape[2]
    return pl.pallas_call(
        functools.partial(kernel, n_doms, n_slabs),
        out_shape=jax.ShapeDtypeStruct((mom, SX, RY, NZ), jnp.float32),
        in_specs=[pl.BlockSpec(memory_space=pl.ANY)] * 5,
        out_specs=pl.BlockSpec(memory_space=pltpu.VMEM),
        scratch_shapes=[
            pltpu.VMEM((blocks, cells, particles), jnp.bfloat16),
            pltpu.VMEM((mom, blocks, particles), jnp.bfloat16),
            pltpu.VMEM((1, blocks), jnp.int32),
            pltpu.VMEM((1, blocks), jnp.int32),
            pltpu.VMEM((1, 1), jnp.int32),
            pltpu.VMEM((mom, blocks, NZ), jnp.float32),
            pltpu.VMEM((n_doms, PLANES, mom, RY, NZ), jnp.float32),
            pltpu.VMEM((n_doms, PLANES, RY, NZ), jnp.float32),
            pltpu.VMEM((n_doms, PLANES, 1, NZ), jnp.float32),
            pltpu.VMEM((n_doms, PLANES, mom // 2, 2 * RY, NZ), jnp.int16),
            pltpu.VMEM((n_doms, PLANES, 1, NZ), jnp.float32),
            pltpu.VMEM((n_doms, PLANES, mom // 2, 2 * RY, NZ), jnp.int16),
            pltpu.SemaphoreType.DMA((4 + LOADS,)),
            pltpu.SemaphoreType.DMA((2, n_doms, len(ORDER))),
            pltpu.SemaphoreType.DMA((2, n_doms, len(ORDER))),
        ],
        compiler_params=pltpu.CompilerParams(
            collective_id=0, has_side_effects=True, vmem_limit_bytes=64 * 1024 * 1024 - 10432 * 1024
        ),
    )(weights, moments.transpose(0, 2, 1, 3), block_tile, block_slab, block_count)


def solution(mesh):
    return jax.shard_map(
        functools.partial(local, mesh.shape["dom"], mesh.shape["slab"]),
        mesh=mesh,
        in_specs=(
            P("slab", "dom", None, None),
            P("slab", "dom", None, None),
            P("slab", "dom"),
            P("slab", "dom"),
            P("slab", "dom"),
        ),
        out_specs=P(None, "slab", "dom", None),
        check_vma=False,
    )
```

```python
import functools

import jax
import jax.numpy as jnp
from jax import lax
from jax.experimental import pallas as pl
from jax.experimental.pallas import tpu as pltpu
from jax.sharding import PartitionSpec as P

SX = 2
RY = 8
NZ = 128
SUB = 16
PLANES = 8
LOADS = 4
LEVELS = 32766.0
SMALLEST = 1e-33
diffusion = 0.16
MESH = pl.DeviceIdType.MESH
RANGES = {-2: (0, 1), -1: (1, 3), 0: (3, 5), 1: (5, 7), 2: (7, 8)}
ORDER = (0, 2, -2, 1, -1)


def in_plane(field, rows):
    count = field.shape[0]
    row = lax.broadcasted_iota(jnp.int32, field.shape, 0) % rows
    lane = lax.broadcasted_iota(jnp.int32, field.shape, 1)
    below = jnp.where(row == 0, 0.0, pltpu.roll(field, 1, 0))
    above = jnp.where(row == rows - 1, 0.0, pltpu.roll(field, count - 1, 0))
    left = jnp.where(lane == 0, 0.0, pltpu.roll(field, 1, 1))
    right = jnp.where(lane == NZ - 1, 0.0, pltpu.roll(field, NZ - 1, 1))
    near = (below + above) + (left + right)
    return (1.0 - 6.0 * diffusion) * field + diffusion * near


def two_passes(field, rows):
    once = in_plane(field, rows)
    twice = in_plane(once, rows) + (2.0 * diffusion * diffusion) * field
    planes = []
    for j in range(PLANES):
        e = j - 2
        total = None
        for source, at, factor in (
            (twice, e, 1.0),
            (once, e - 1, 2.0 * diffusion),
            (once, e + 1, 2.0 * diffusion),
            (field, e - 2, diffusion * diffusion),
            (field, e + 2, diffusion * diffusion),
        ):
            if 0 <= at < SX + 2:
                part = factor * source[at * rows : (at + 1) * rows]
                total = part if total is None else total + part
        planes.append(total)
    return planes


def kernel(
    n_doms, n_slabs,
    w_hbm, m_hbm, tile_hbm, slab_hbm, count_hbm, out_ref,
    w_ref, m_ref, tile_ref, slab_ref, count_ref,
    terms, fields, peaks, send_scale, send_level, recv_scale, recv_level,
    load_sem, send_sem, recv_sem,
):
    my_dom = lax.axis_index("dom")
    my_slab = lax.axis_index("slab")
    moments, blocks, particles = m_ref.shape
    cells = w_ref.shape[1]
    pairs = [(tile_hbm, tile_ref), (slab_hbm, slab_ref), (count_hbm, count_ref), (m_hbm.at[0], m_ref)]
    for g in range(LOADS):
        part = pl.ds(g * (blocks // LOADS), blocks // LOADS)
        pairs.append((w_hbm.at[0, part], w_ref.at[part]))
    loads = [
        pltpu.make_async_copy(src, dst, load_sem.at[i]) for i, (src, dst) in enumerate(pairs)
    ]
    for load in loads:
        load.start()

    peers = [(k, ds) for k in range(n_doms) for ds in ORDER if k or ds]

    def peer(k, ds):
        return (lax.rem(my_dom + k, n_doms), lax.rem(my_slab + ds + n_slabs, n_slabs))

    barrier = pltpu.get_barrier_semaphore()
    for k, ds in peers:
        pl.semaphore_signal(barrier, inc=1, device_id=peer(k, ds), device_id_type=MESH)

    for load in loads[:3]:
        load.wait()
    rows = RY * n_doms
    plane_tiles = rows * (NZ // cells)
    half_rows = (SX + 2) * rows

    tile = tile_ref[...]
    step = slab_ref[...] - my_slab
    ahead = jnp.logical_or(step == 1, step == 1 - n_slabs)
    behind = jnp.logical_or(step == -1, step == n_slabs - 1)
    shift = jnp.where(ahead, SX + 1, jnp.where(behind, 1 - SX, 1)) * plane_tiles
    ext = tile + shift
    ext = (ext & 1) * half_rows + (ext >> 1)
    slot = lax.broadcasted_iota(jnp.int32, ext.shape, 1)
    ext = jnp.where(slot < count_ref[...], ext, -1)
    place = lax.broadcasted_iota(jnp.int32, (2 * half_rows, blocks), 0)
    hot = jnp.where(place == ext, 1.0, 0.0).astype(jnp.bfloat16)

    row = lax.broadcasted_iota(jnp.int32, (8, NZ), 0)
    lane = lax.broadcasted_iota(jnp.int32, (8, NZ), 1)
    in_place = (row % 2 == 0) == (lane < cells)
    loads[3].wait()
    for g in range(blocks // SUB):
        share = LOADS * SUB // blocks
        for load in loads[4 + share * g : 4 + share * (g + 1)]:
            load.wait()
        left = m_ref[:, SUB * g : SUB * (g + 1), :].reshape(moments * SUB, particles)
        right = w_ref[SUB * g : SUB * (g + 1)].reshape(SUB * cells, particles)
        product = lax.dot_general(
            left, right, (((1,), (1,)), ((), ())), preferred_element_type=jnp.float32
        )
        for m in range(moments):
            for h in range(2):
                top = SUB * m + 8 * h
                piece = None
                for pair in range(4):
                    at = NZ * (4 * h + pair)
                    found = product[top : top + 8, at : at + NZ]
                    piece = found if piece is None else jnp.where(row // 2 == pair, found, piece)
                both = jnp.where(in_place, piece, pltpu.roll(piece, NZ // 2, 1))
                terms[m, SUB * g + 8 * h : SUB * g + 8 * (h + 1), :] = both

    wide = lax.broadcasted_iota(jnp.int32, (half_rows, NZ), 1) < cells
    for m in range(moments):
        term = terms[m]
        total = None
        for _ in range(2):
            part = term.astype(jnp.bfloat16)
            term = term - part.astype(jnp.float32)
            added = jnp.dot(hot, part, preferred_element_type=jnp.float32)
            total = added if total is None else total + added
        field = jnp.where(wide, total[:half_rows], total[half_rows:])
        planes = two_passes(field, rows)
        for j in range(PLANES):
            for d in range(n_doms):
                block = planes[j][RY * d : RY * (d + 1)]
                fields[d, j, m] = block
                peak = jnp.abs(block)
                peaks[d, j] = peak if m == 0 else jnp.maximum(peaks[d, j], peak)

    copies = []
    for n, ds in enumerate(ORDER):
        first, last = RANGES[ds]
        for d in range(n_doms):
            for j in range(first, last):
                peak = jnp.maximum(jnp.max(peaks[d, j], axis=0, keepdims=True), SMALLEST)
                send_scale[d, j] = peak * (1.0 / LEVELS)
                inverse = LEVELS / peak
                for p in range(moments // 2):
                    pair = fields[d, j, 2 * p : 2 * p + 2].reshape(2 * RY, NZ)
                    level = jnp.round(pair * inverse).astype(jnp.int32)
                    send_level[d, j, p] = level.astype(jnp.int16)
        if n == 0:
            pl.semaphore_wait(barrier, len(peers))
        span = pl.ds(first, last - first)
        for k in reversed(range(n_doms)):
            if k == 0 and ds == 0:
                continue
            target = peer(k, ds)
            group = []
            for i, (source, landing) in enumerate(
                ((send_scale, recv_scale), (send_level, recv_level))
            ):
                copy = pltpu.make_async_remote_copy(
                    src_ref=source.at[target[0], span],
                    dst_ref=landing.at[k, span],
                    send_sem=send_sem.at[i, k, n],
                    recv_sem=recv_sem.at[i, k, n],
                    device_id=target,
                    device_id_type=MESH,
                )
                copy.start()
                group.append(copy)
            copies.append((k, ds, group))

    own = fields.at[my_dom]
    sums = [own[4], own[3]]
    for k, ds, group in reversed(copies):
        for copy in group:
            copy.wait_recv()
        for j in range(*RANGES[ds]):
            level = recv_level[k, j].astype(jnp.float32).reshape(moments, RY, NZ)
            sums[j % 2] = sums[j % 2] + level * recv_scale[k, j]
    out_ref[:, 0] = sums[1]
    out_ref[:, 1] = sums[0]
    for _, _, group in copies:
        for copy in group:
            copy.wait_send()


def local(n_doms, n_slabs, weights, moments, block_tile, block_slab, block_count):
    _, blocks, cells, particles = weights.shape
    mom = moments.shape[2]
    return pl.pallas_call(
        functools.partial(kernel, n_doms, n_slabs),
        out_shape=jax.ShapeDtypeStruct((mom, SX, RY, NZ), jnp.float32),
        in_specs=[pl.BlockSpec(memory_space=pl.ANY)] * 5,
        out_specs=pl.BlockSpec(memory_space=pltpu.VMEM),
        scratch_shapes=[
            pltpu.VMEM((blocks, cells, particles), jnp.bfloat16),
            pltpu.VMEM((mom, blocks, particles), jnp.bfloat16),
            pltpu.VMEM((1, blocks), jnp.int32),
            pltpu.VMEM((1, blocks), jnp.int32),
            pltpu.VMEM((1, 1), jnp.int32),
            pltpu.VMEM((mom, blocks, NZ), jnp.float32),
            pltpu.VMEM((n_doms, PLANES, mom, RY, NZ), jnp.float32),
            pltpu.VMEM((n_doms, PLANES, RY, NZ), jnp.float32),
            pltpu.VMEM((n_doms, PLANES, 1, NZ), jnp.float32),
            pltpu.VMEM((n_doms, PLANES, mom // 2, 2 * RY, NZ), jnp.int16),
            pltpu.VMEM((n_doms, PLANES, 1, NZ), jnp.float32),
            pltpu.VMEM((n_doms, PLANES, mom // 2, 2 * RY, NZ), jnp.int16),
            pltpu.SemaphoreType.DMA((4 + LOADS,)),
            pltpu.SemaphoreType.DMA((2, n_doms, len(ORDER))),
            pltpu.SemaphoreType.DMA((2, n_doms, len(ORDER))),
        ],
        compiler_params=pltpu.CompilerParams(
            collective_id=0, has_side_effects=True, vmem_limit_bytes=64 * 1024 * 1024 - 10432 * 1024
        ),
    )(weights, moments.transpose(0, 2, 1, 3), block_tile, block_slab, block_count)


def solution(mesh):
    return jax.shard_map(
        functools.partial(local, mesh.shape["dom"], mesh.shape["slab"]),
        mesh=mesh,
        in_specs=(
            P("slab", "dom", None, None),
            P("slab", "dom", None, None),
            P("slab", "dom"),
            P("slab", "dom"),
            P("slab", "dom"),
        ),
        out_specs=P(None, "slab", "dom", None),
        check_vma=False,
    )
```
